32 devices in a mesh: lat: 4 (over z), lon: 8 (over y, x, core).
Axes of the slice: x: 2, y: 2, z: 4, core: 2. Of those that a mesh axis runs over, the one named last changes fastest.
Arguments:
- control: float32 [64, 64, 1024], P(None, 'lat', 'lon'), may hold values from -6 to 6
- kappa: float32 [2, 64, 1024], P(None, 'lat', 'lon'), may hold values from 0.08 to 0.24
- vert_sqrt: float32 [64, 64], replicated, may hold values from -0.75 to 0.75
- obs_tile: int32 [65536, 1], P(('lat', 'lon')), may hold values from 0 to 31; in each aligned block of 2048 rows (0 to 2047, 2048 to 4095, ...) at most 128 rows name the same one
- obs_cell: int32 [65536], P(('lat', 'lon')), may hold values from 0 to 2047
- obs_frac: float32 [2, 65536], P(None, ('lat', 'lon')), may hold values from 0 to 1
- obs_value: float32 [64, 65536], P(None, ('lat', 'lon')), may hold values from -6 to 6
- obs_precision: float32 [64, 65536], P(None, ('lat', 'lon')), may hold values from 0.25 to 4
Outputs:
- gradient: float32 [64, 64, 1024], P(None, 'lat', 'lon')
The draws below stay inside these ranges and needn't reach their ends.
Inputs may be any that keep to these rules, and one draw needn't show every extreme that they name: `obs_tile`: among the profiles of one device, no tile is named by more than 128; some tile is named by exactly 128.
All inputs are finite; a program needn't handle non-finite values.
Results may differ from the reference program's by a relative error of at most 0.000067.
Values sent between devices are 32-bit elements; how exact they have to be, the bound alone decides.
A program may use at most 128 MiB of HBM per device.

```python
import math
import jax
import jax.numpy as jnp
import numpy as np
from jax import lax

LEV = 64
CLAT = 16
CLON = 128
OBS_DEV = 2048
STEPS = 4
NLAT = 64
NLON = 1024
OBS = 65536
CAP = 128
N_LON = 8
DEVICES = 32


def draw_kappa(key, part):
    unit = jax.random.uniform(key, (2, NLAT, NLON), jnp.float32)
    return 0.08 * jnp.exp(unit * jnp.log(3.0))


def touch_ends(result, stream_key, least, top_value):
    longest = result.shape.index(max(result.shape))
    spots = []
    for shift in (0, 1):
        where = [jax.random.randint(jax.random.fold_in(stream_key, axis), (), 0, length) for axis, length in enumerate(result.shape)]
        where[longest] = (where[longest] + shift) % result.shape[longest]
        spots.append(tuple(where))
    return result.at[spots[0]].set(least).at[spots[1]].set(top_value)


def block_levels(rng, extent, shards, smallest, largest):
    level, own = 1.0, jax.random.fold_in(rng, 6)
    for position, blocks in shards:
        steps = jnp.exp(jax.random.uniform(jax.random.fold_in(own, position), (blocks,), jnp.float32, smallest / len(shards), largest / len(shards)))
        level = level * jnp.repeat(steps, extent[position] // blocks).reshape([-1 if axis == position else 1 for axis in range(len(extent))])
    return level


def routed_block(own_key, own, number, rows, count, top, most, lean):
    sequence = jax.random.permutation(own_key, count)
    heavy_load, common = load_shares(count, rows * top, most, lean, True), load_shares(count, rows * top, most, lean, False)
    places = jnp.arange(count)

    def named(lengths, offset_by):
        used = int((lengths > 0).sum())
        fixed = max(1, used // 4)
        passed = fixed + (places - fixed + offset_by * (used - fixed)) % max(1, count - fixed)
        return jnp.zeros((count,), jnp.int32).at[sequence[jnp.where(places < fixed, places, passed)]].set(jnp.asarray(lengths, jnp.int32))

    lengths = jnp.where(number % 4 == 0, named(heavy_load, number // 4), named(common, number - number // 4 - 1))
    mixed = jax.random.permutation(jax.random.fold_in(own, 3), count)
    source_of, sink = mixed[0:count // 2 * 2:2], mixed[1:count // 2 * 2:2]
    room = jnp.minimum(lengths[source_of] - 1, most - lengths[sink]) // 2
    room = jnp.where((source_of == sequence[0]) | (sink == sequence[0]) | (lengths[sink] == 0), 0, jnp.maximum(room, 0))
    passed = jax.random.randint(jax.random.fold_in(own, 4), (count // 2,), 0, 1 << 20) % (room + 1)
    lengths = lengths.at[source_of].add(-passed).at[sink].add(passed)
    members = jnp.searchsorted(jnp.cumsum(lengths), jnp.arange(rows * top), side="right").astype(jnp.int32)
    grid = members.reshape(top, rows).T
    grid = grid[jax.random.permutation(jax.random.fold_in(own, 1), rows)]
    offset_by = jax.random.randint(jax.random.fold_in(own, 2), (rows, 1), 0, top)
    return jnp.take_along_axis(grid, (jnp.arange(top)[None, :] + offset_by) % top, axis=1)


def load_shares(number_of, total, limit, lean, full):
    weights = [(1 << 20) // math.isqrt(grade ** lean) + 1 for grade in range(1, number_of + 1)]
    largest = limit if full else min(limit, max(-(-total // number_of), total * weights[0] // sum(weights)))
    least = 1 if total - largest >= number_of - 1 else 0
    given, spare = [largest] + [least] * (number_of - 1), total - largest - least * (number_of - 1)
    while spare > 0:
        movable = [i for i in range(1, number_of) if given[i] < largest] or [i for i in range(1, number_of) if given[i] < limit]
        pool, budget = sum([weights[i] for i in movable]), spare
        for i in movable:
            addition = min(limit - given[i], max(1, budget * weights[i] // pool), spare)
            given[i] = given[i] + addition
            spare = spare - addition
    return np.array(given)


def scatter_about(rng, shape, spread, limit, pieces=(), kind=jnp.bfloat16):
    gain = block_levels(rng, shape, pieces, -0.22, 0.18) if pieces else 1.0
    result = jax.random.normal(rng, shape, jnp.float32) * spread * gain
    return jnp.minimum(jnp.maximum(result, -limit), limit).astype(kind)


def setup_inputs(seed: int = 0) -> dict:
    key_of = jax.random.split(jax.random.key(seed), 9)
    control = scatter_about(key_of[0], (LEV, NLAT, NLON), 1.0, 6.0, ((1, 4), (2, 8)), jnp.float32)
    kappa = draw_kappa(jax.random.fold_in(key_of[8], 71), 0)
    vert_sqrt = scatter_about(key_of[2], (LEV, LEV), LEV ** -0.5, 0.75, (), jnp.float32)
    obs_tile_keys = jax.random.split(jax.random.fold_in(key_of[3], 1), OBS // OBS_DEV)
    obs_tile_turns = jax.random.permutation(jax.random.fold_in(key_of[3], 3), OBS // OBS_DEV)
    obs_tile = jax.vmap(lambda own, number: routed_block(jax.random.fold_in(key_of[3], 2), own, number, OBS_DEV, DEVICES, 1, CAP, 2))(obs_tile_keys, obs_tile_turns).reshape((OBS, 1))
    obs_cell = touch_ends(jax.random.randint(key_of[4], (OBS,), 0, CLAT * CLON), jax.random.fold_in(key_of[4], 1), 0, (CLAT * CLON) - 1).astype(jnp.int32)
    obs_frac = jnp.clip(1.0 * jax.random.uniform(key_of[5], (2, OBS), jnp.float32) ** block_levels(key_of[5], (2, OBS), ((1, 32),), -0.2, 0.2), 0.0, 1.0)
    obs_value = scatter_about(key_of[6], (LEV, OBS), 1.0, 6.0, ((1, 32),), jnp.float32)
    obs_precision = jnp.clip(jnp.exp(math.log(4.0) - 2.7725887 * jax.random.uniform(key_of[7], (LEV, OBS), jnp.float32) ** block_levels(key_of[7], (LEV, OBS), ((1, 32),), -0.2, 0.2)), 0.25, 4.0)
    return {"control": control, "kappa": kappa, "vert_sqrt": vert_sqrt, "obs_tile": obs_tile, "obs_cell": obs_cell, "obs_frac": obs_frac, "obs_value": obs_value, "obs_precision": obs_precision}


def diffuse_level(plane, lon_coef, lat_coef):
    zero_row = jnp.zeros((1, plane.shape[1]), jnp.float32)
    west_coef = jnp.roll(lon_coef, 1, axis=1)
    south_coef = jnp.concatenate([zero_row, lat_coef[:-1]], 0)
    for _ in range(STEPS):
        east_val = jnp.roll(plane, -1, axis=1)
        west_val = jnp.roll(plane, 1, axis=1)
        north_val = jnp.concatenate([plane[1:], zero_row], 0)
        south_val = jnp.concatenate([zero_row, plane[:-1]], 0)
        plane = plane + lon_coef * (east_val - plane) + west_coef * (west_val - plane) + lat_coef * (north_val - plane) + south_coef * (south_val - plane)
    return plane

def smooth_all(field, kappa):
    row_ids = jnp.arange(NLAT)
    lat_coef = kappa[1] * (row_ids < NLAT - 1).astype(jnp.float32)[:, None]
    lon_coef = kappa[0]
    return lax.map(lambda plane: diffuse_level(plane, lon_coef, lat_coef), field)

def reference(control, kappa, vert_sqrt, obs_tile, obs_cell, obs_frac, obs_value, obs_precision):
    smoothed = smooth_all(control, kappa)
    state = jnp.dot(vert_sqrt, smoothed.reshape(LEV, -1), precision=lax.Precision.HIGHEST, preferred_element_type=jnp.float32).reshape(LEV, NLAT, NLON)
    extended = jnp.concatenate([state, jnp.zeros((LEV, 1, NLON), jnp.float32)], 1)
    tile_ids = obs_tile[:, 0]
    row_of = tile_ids // N_LON * CLAT + obs_cell // CLON
    col_of = tile_ids % N_LON * CLON + obs_cell % CLON
    col_next = (col_of + 1) % NLON
    row_next = row_of + 1
    east_frac = obs_frac[0]
    north_frac = obs_frac[1]
    corners = [(row_of, col_of, (1.0 - east_frac) * (1.0 - north_frac)), (row_of, col_next, east_frac * (1.0 - north_frac)), (row_next, col_of, (1.0 - east_frac) * north_frac), (row_next, col_next, east_frac * north_frac)]
    model_obs = jnp.zeros((LEV, obs_cell.shape[0]), jnp.float32)
    for row_at, col_at, share in corners:
        model_obs = model_obs + share[None, :] * extended[:, row_at, col_at]
    weighted = obs_precision * (model_obs - obs_value)
    adjoint = jnp.zeros((LEV, NLAT + 1, NLON), jnp.float32)
    for row_at, col_at, share in corners:
        adjoint = adjoint.at[:, row_at, col_at].add(share[None, :] * weighted)
    adjoint = adjoint[:, :NLAT]
    back = jnp.dot(vert_sqrt.T, adjoint.reshape(LEV, -1), precision=lax.Precision.HIGHEST, preferred_element_type=jnp.float32).reshape(LEV, NLAT, NLON)
    return control + smooth_all(back, kappa)
```

```python
import functools

import jax
import jax.numpy as jnp
from jax import lax
from jax.experimental import pallas as pl
from jax.experimental.pallas import tpu as pltpu
from jax.sharding import PartitionSpec as P

STEPS = 4
ROWS_SENT = 136
MESH = pl.DeviceIdType.MESH
SIDES = ((0, 1), (0, -1), (1, 1), (1, -1), (-1, 1), (-1, -1))
NT = (((1,), (1,)), ((), ()))
BF = jnp.bfloat16
F32 = jnp.float32


def split_two(x):
    hi = x.astype(BF)
    return hi, (x - hi.astype(F32)).astype(BF)


def pack_kernel(tiles, cap, tile_ref, cell_ref, frac_ref, value_ref, prec_ref, out_ref, pay_ref, slot_ref):
    lev, count = value_ref.shape
    tile = tile_ref[...]
    named = (lax.broadcasted_iota(jnp.int32, (tiles, count), 0) == tile).astype(F32)
    width = 256
    upper = (
        lax.broadcasted_iota(jnp.int32, (width, width), 0)
        < lax.broadcasted_iota(jnp.int32, (width, width), 1)
    ).astype(F32).astype(BF)
    carry = jnp.zeros((tiles, 1), F32)
    for first in range(0, count, width):
        part = named[:, first : first + width]
        before = jnp.dot(part.astype(BF), upper, preferred_element_type=F32) + carry
        rank = jnp.sum(before * part, axis=0, keepdims=True)
        slot_ref[:, first : first + width] = (
            tile[:, first : first + width] * cap + rank.astype(jnp.int32)
        )
        carry = carry + jnp.sum(part, axis=1, keepdims=True)
    tail = jnp.concatenate(
        [frac_ref[...], cell_ref[...].astype(F32), jnp.zeros((13, count), F32)], 0
    )
    at = 0
    for piece in (value_ref[...], prec_ref[...], tail):
        hi, lo = split_two(piece)
        n = piece.shape[0]
        pay_ref[at : at + n, :] = hi
        pay_ref[144 + at : 144 + at + n, :] = lo
        at += n
    group = 256 // cap
    slots = slot_ref[...]

    def body(g, _):
        ids = lax.broadcasted_iota(jnp.int32, (256, count), 0) + g * 256
        hot = (ids == slots).astype(F32).astype(BF)
        got = lax.dot_general(pay_ref[...], hot, NT, preferred_element_type=F32)
        both = got[:ROWS_SENT] + got[144 : 144 + ROWS_SENT]
        for j in range(group):
            out_ref[g * group + j] = both[:, j * cap : (j + 1) * cap]
        return 0

    lax.fori_loop(0, tiles // group, body, 0)


def main_kernel(
    n_lat, n_lon, send_ref, control_ref, kappa_ref, vert_ref, vert_t_ref, out_ref,
    recv, ext, side, edges, near, coef, wide, s4, a4, row_out, row_in, col_out, col_in,
    ext2, side2, edges2, near2,
    a_send, a_recv, own_sem, lat_send, lat_recv, lon_send, lon_recv, st_send, st_recv,
    ad_send, ad_recv, lat2_send, lat2_recv, lon2_send, lon2_recv,
):
    devices, _, cap = recv.shape
    lev, rows, cols = control_ref.shape
    lat, lon = lax.axis_index("lat"), lax.axis_index("lon")
    me = lat * n_lon + lon
    top = lat == n_lat - 1
    bottom = lat == 0

    def to(dy, dx):
        return (lax.rem(lat + dy + n_lat, n_lat), lax.rem(lon + dx + n_lon, n_lon))

    def at_distance(k):
        d = lax.rem(me + k, devices)
        return d // n_lon, lax.rem(d, n_lon), d

    barrier = pltpu.get_barrier_semaphore()

    def greet(k, _):
        y, x, _d = at_distance(k)
        pl.semaphore_signal(barrier, inc=1, device_id=(y, x), device_id_type=MESH)
        return 0

    lax.fori_loop(1, devices, greet, 0)
    pl.semaphore_wait(barrier, devices - 1)

    def obs_copy(k):
        y, x, d = at_distance(k)
        return pltpu.make_async_remote_copy(
            src_ref=send_ref.at[d], dst_ref=recv.at[k], send_sem=a_send.at[k],
            recv_sem=a_recv.at[k], device_id=(y, x), device_id_type=MESH,
        )

    lane = lax.broadcasted_iota(jnp.int32, (1, cols), 1)

    def edge_block(values):
        acc = jnp.zeros(values[0].shape, F32)
        for r, x in enumerate(values):
            acc = jnp.where((lane >= 4 * r) & (lane < 4 * r + 4), pltpu.roll(x, (4 * r + 4) % cols, 1), acc)
            b = 64 + 4 * r
            acc = jnp.where((lane >= b) & (lane < b + 4), pltpu.roll(x, b % cols, 1), acc)
        return acc

    def halo_copies(ext_, edges_, near_, sems):
        ls, lr, os, orr = sems
        copies = [
            pltpu.make_async_remote_copy(
                src_ref=ext_.at[pl.ds(4, 4)], dst_ref=ext_.at[pl.ds(rows + 4, 4)], send_sem=ls.at[0],
                recv_sem=lr.at[0], device_id=to(-1, 0), device_id_type=MESH),
            pltpu.make_async_remote_copy(
                src_ref=ext_.at[pl.ds(rows, 4)], dst_ref=ext_.at[pl.ds(0, 4)], send_sem=ls.at[1],
                recv_sem=lr.at[1], device_id=to(1, 0), device_id_type=MESH),
        ]
        for j, (dy, dx) in enumerate(SIDES):
            copies.append(pltpu.make_async_remote_copy(
                src_ref=edges_, dst_ref=near_.at[j], send_sem=os.at[j], recv_sem=orr.at[j],
                device_id=to(-dy, -dx), device_id_type=MESH))
        return copies

    def build_side(near_, side_):
        for r in range(rows + 8):
            q = r - 4
            dy = 0 if 0 <= q < rows else (-1 if q < 0 else 1)
            rr = q - dy * rows
            east = near_[SIDES.index((dy, 1))]
            west = near_[SIDES.index((dy, -1))]
            side_[r] = jnp.where(
                lane < 4, pltpu.roll(east, (cols - 64 - 4 * rr) % cols, 1),
                jnp.where(lane >= cols - 4, pltpu.roll(west, (cols - 4 - 4 * rr) % cols, 1), 0.0))

    def ring(m, s, step):
        shift = 1 if step < 0 else cols - 1
        edge = lane == (0 if step < 0 else cols - 1)
        rm, rs = pltpu.roll(m, shift, 1), pltpu.roll(s, shift, 1)
        return jnp.where(edge, rs, rm), jnp.where(edge, rm, rs)

    def smooth(main_, side_, put):
        def body(b, _):
            lv = pl.ds(pl.multiple_of(b * 8, 8), 8)
            m = [main_[r, lv, :] for r in range(rows + 8)]
            s = [side_[r, lv, :] for r in range(rows + 8)]
            for step in range(STEPS):
                nm, ns = list(m), list(s)
                for r in range(step + 1, rows + 7 - step):
                    em, es = ring(m[r], s[r], 1)
                    wm, ws = ring(m[r], s[r], -1)
                    nm[r] = (coef[0, r] * m[r] + coef[1, r] * em + coef[2, r] * wm
                             + coef[3, r] * m[r + 1] + coef[3, r - 1] * m[r - 1])
                    if step < STEPS - 1:
                        ns[r] = (coef[4, r] * s[r] + coef[5, r] * es + coef[6, r] * ws
                                 + coef[7, r] * s[r + 1] + coef[7, r - 1] * s[r - 1])
                m, s = nm, ns
            for r in range(rows):
                put(lv, r, m[r + 4])
            return 0

        lax.fori_loop(0, lev // 8, body, 0)

    zero6 = jnp.zeros((6, cols), F32)
    for r in range(rows):
        ext[r + 4, 0:lev, :] = control_ref[:, r, :]
        north = kappa_ref[1, r : r + 1, :]
        if r == rows - 1:
            north = jnp.where(top, 0.0, north)
        ext[r + 4, lev : lev + 8, :] = jnp.concatenate([kappa_ref[0, r : r + 1, :], north, zero6], 0)
    edges[...] = edge_block([ext[r + 4] for r in range(rows)])
    first = halo_copies(ext, edges, near, (lat_send, lat_recv, lon_send, lon_recv))
    for c in first:
        c.start()

    def start_obs(k, _):
        obs_copy(k).start()
        return 0

    lax.fori_loop(1, devices, start_obs, 0)
    own = pltpu.make_async_copy(send_ref.at[me], recv.at[0], own_sem)
    own.start()
    for c in first:
        c.wait()
    build_side(near, side)

    def spread(x):
        return jnp.broadcast_to(x, (8, cols))

    for r in range(rows + 8):
        km, ks = ext[r, lev : lev + 8, :], side[r, lev : lev + 8, :]
        em, es = spread(km[0:1]), spread(ks[0:1])
        wm, ws = ring(em, es, -1)
        nm, ns = spread(km[1:2]), spread(ks[1:2])
        coef[1, r], coef[2, r], coef[3, r] = em, wm, nm
        coef[5, r], coef[6, r], coef[7, r] = es, ws, ns
        if r:
            coef[0, r] = 1.0 - em - wm - nm - coef[3, r - 1]
            coef[4, r] = 1.0 - es - ws - ns - coef[7, r - 1]

    def put_wide(lv, r, x):
        wide[lv, r * cols : (r + 1) * cols] = x

    smooth(ext, side, put_wide)
    wide[...] = jnp.dot(vert_ref[...], wide[...], precision=lax.Precision.HIGHEST, preferred_element_type=F32)

    def row(r):
        return wide[:, r * cols : (r + 1) * cols]

    row_out[0] = row(0)
    acc = jnp.zeros((lev, cols), F32)
    for r in range(rows):
        acc = jnp.where(lane == r, pltpu.roll(row(r), r, 1), acc)
    col_out[0] = acc

    def trio(which, sign, sems, semr):
        return [
            pltpu.make_async_remote_copy(
                src_ref=row_out.at[which], dst_ref=row_in.at[which], send_sem=sems.at[0], recv_sem=semr.at[0],
                device_id=to(sign, 0), device_id_type=MESH),
            pltpu.make_async_remote_copy(
                src_ref=col_out.at[which], dst_ref=col_in.at[which, 0], send_sem=sems.at[1], recv_sem=semr.at[1],
                device_id=to(0, sign), device_id_type=MESH),
            pltpu.make_async_remote_copy(
                src_ref=col_out.at[which], dst_ref=col_in.at[which, 1], send_sem=sems.at[2], recv_sem=semr.at[2],
                device_id=to(sign, sign), device_id_type=MESH),
        ]

    second = trio(0, -1, st_send, st_recv)
    for c in second:
        c.start()
    for c in second:
        c.wait()
    last_row = jnp.where(top, 0.0, row_in[0])
    last_corner = jnp.where(top, 0.0, col_in[0, 1])

    def put_s4(corner, r, x):
        hi, lo = split_two(x)
        s4[corner * lev : (corner + 1) * lev, r * cols : (r + 1) * cols] = hi
        s4[(corner + 4) * lev : (corner + 5) * lev, r * cols : (r + 1) * cols] = lo

    for r in range(rows + 1):
        x = row(r) if r < rows else last_row
        over = pltpu.roll(col_in[0, 0], cols - 1 - r, 1) if r < rows else pltpu.roll(last_corner, cols - 1, 1)
        e = jnp.where(lane == cols - 1, over, pltpu.roll(x, cols - 1, 1))
        if r < rows:
            put_s4(0, r, x)
            put_s4(1, r, e)
        if r:
            put_s4(2, r - 1, x)
            put_s4(3, r - 1, e)

    a4[...] = jnp.zeros_like(a4)
    own.wait()
    group = max(1, 256 // cap)

    def work(g, _):
        for j in range(group):
            k = g * group + j

            @pl.when(k > 0)
            def _():
                obs_copy(k).wait_recv()

        got = jnp.concatenate([recv[g * group + j] for j in range(group)], 1)
        fx, fy = got[2 * lev : 2 * lev + 1], got[2 * lev + 1 : 2 * lev + 2]
        cell = got[2 * lev + 2 : 2 * lev + 3].astype(jnp.int32)
        hot = (lax.broadcasted_iota(jnp.int32, (rows * cols, group * cap), 0) == cell).astype(F32).astype(BF)
        m4 = jnp.dot(s4[...], hot, preferred_element_type=F32)
        shares = ((1.0 - fx) * (1.0 - fy), fx * (1.0 - fy), (1.0 - fx) * fy, fx * fy)
        model = jnp.zeros((lev, group * cap), F32)
        for c, w in enumerate(shares):
            model = model + w * (m4[c * lev : (c + 1) * lev] + m4[(c + 4) * lev : (c + 5) * lev])
        weighted = got[lev : 2 * lev] * (model - got[:lev])
        hi, lo = split_two(jnp.concatenate([w * weighted for w in shares], 0))
        a4[...] += (lax.dot_general(hi, hot, NT, preferred_element_type=F32)
                    + lax.dot_general(lo, hot, NT, preferred_element_type=F32))
        return 0

    lax.fori_loop(0, devices // group, work, 0)

    def part(c, r):
        return a4[c * lev : (c + 1) * lev, r * cols : (r + 1) * cols]

    here, above, packed = [], [], jnp.zeros((lev, cols), F32)
    for r in range(rows):
        e0, e1 = pltpu.roll(part(1, r), 1, 1), pltpu.roll(part(3, r), 1, 1)
        here.append(part(0, r) + jnp.where(lane == 0, 0.0, e0))
        above.append(part(2, r) + jnp.where(lane == 0, 0.0, e1))
        packed = packed + jnp.where(lane == r, pltpu.roll(e0, r, 1), 0.0)
        packed = packed + jnp.where(lane == r + 1, pltpu.roll(e1, r + 1, 1), 0.0)
        wide[:, r * cols : (r + 1) * cols] = here[r] + above[r - 1] if r else here[r]
    row_out[1] = above[rows - 1]
    col_out[1] = packed
    third = trio(1, 1, ad_send, ad_recv)
    for c in third:
        c.start()
    for c in third:
        c.wait()
    wide[:, 0:cols] += (jnp.where(bottom, 0.0, row_in[1])
                        + jnp.where((lane == 0) & jnp.logical_not(bottom), pltpu.roll(col_in[1, 1], cols - rows, 1), 0.0))
    for r in range(rows):
        wide[:, r * cols : (r + 1) * cols] += jnp.where(
            lane == 0, pltpu.roll(col_in[1, 0], (cols - r) % cols, 1), 0.0)
    back = jnp.dot(vert_t_ref[...], wide[...], precision=lax.Precision.HIGHEST, preferred_element_type=F32)
    for r in range(rows):
        ext2[r + 4] = back[:, r * cols : (r + 1) * cols]
    edges2[...] = edge_block([ext2[r + 4] for r in range(rows)])
    fourth = halo_copies(ext2, edges2, near2, (lat2_send, lat2_recv, lon2_send, lon2_recv))
    for c in fourth:
        c.start()
    for c in fourth:
        c.wait()
    build_side(near2, side2)

    def put_out(lv, r, x):
        out_ref[lv, r, :] = x

    smooth(ext2, side2, put_out)

    def end_obs(k, _):
        obs_copy(k).wait_send()
        return 0

    lax.fori_loop(1, devices, end_obs, 0)


def per_device(control, kappa, vert_sqrt, obs_tile, obs_cell, obs_frac, obs_value, obs_precision):
    lev, rows, cols = control.shape
    n_lat, n_lon = lax.axis_size("lat"), lax.axis_size("lon")
    devices = n_lat * n_lon
    count = obs_cell.shape[0]
    cap = 2 * count // devices
    vmem = pl.BlockSpec(memory_space=pltpu.VMEM)
    send = pl.pallas_call(
        functools.partial(pack_kernel, devices, cap),
        out_shape=jax.ShapeDtypeStruct((devices, ROWS_SENT, cap), F32),
        in_specs=[vmem] * 5,
        out_specs=vmem,
        scratch_shapes=[pltpu.VMEM((288, count), BF), pltpu.VMEM((1, count), jnp.int32)],
        compiler_params=pltpu.CompilerParams(vmem_limit_bytes=48 * 2**20),
        name="pack",
    )(obs_tile.reshape(1, count), obs_cell.reshape(1, count), obs_frac, obs_value, obs_precision)
    dma = pltpu.SemaphoreType.DMA
    smoothed = pl.pallas_call(
        functools.partial(main_kernel, n_lat, n_lon),
        out_shape=jax.ShapeDtypeStruct((lev, rows, cols), F32),
        in_specs=[pl.BlockSpec(memory_space=pl.ANY)] + [vmem] * 4,
        out_specs=vmem,
        scratch_shapes=[
            pltpu.VMEM((devices, ROWS_SENT, cap), F32),
            pltpu.VMEM((rows + 8, lev + 8, cols), F32),
            pltpu.VMEM((rows + 8, lev + 8, cols), F32),
            pltpu.VMEM((lev + 8, cols), F32),
            pltpu.VMEM((6, lev + 8, cols), F32),
            pltpu.VMEM((8, rows + 8, 8, cols), F32),
            pltpu.VMEM((lev, rows * cols), F32),
            pltpu.VMEM((8 * lev, rows * cols), BF),
            pltpu.VMEM((4 * lev, rows * cols), F32),
            pltpu.VMEM((2, lev, cols), F32),
            pltpu.VMEM((2, lev, cols), F32),
            pltpu.VMEM((2, lev, cols), F32),
            pltpu.VMEM((2, 2, lev, cols), F32),
            pltpu.VMEM((rows + 8, lev, cols), F32),
            pltpu.VMEM((rows + 8, lev, cols), F32),
            pltpu.VMEM((lev, cols), F32),
            pltpu.VMEM((6, lev, cols), F32),
            dma((devices,)), dma((devices,)), dma,
            dma((2,)), dma((2,)), dma((6,)), dma((6,)),
            dma((3,)), dma((3,)), dma((3,)), dma((3,)),
            dma((2,)), dma((2,)), dma((6,)), dma((6,)),
        ],
        compiler_params=pltpu.CompilerParams(
            collective_id=0, has_side_effects=True, vmem_limit_bytes=48 * 2**20),
        name="main",
    )(send, control, kappa, vert_sqrt, vert_sqrt.T)
    return control + smoothed


def solution(mesh):
    in_specs = (
        P(None, "lat", "lon"), P(None, "lat", "lon"), P(), P(("lat", "lon"), None), P(("lat", "lon")),
        P(None, ("lat", "lon")), P(None, ("lat", "lon")), P(None, ("lat", "lon")),
    )
    return jax.shard_map(
        per_device, mesh=mesh, in_specs=in_specs, out_specs=P(None, "lat", "lon"), check_vma=False
    )
```

```python
import functools

import jax
import jax.numpy as jnp
from jax import lax
from jax.experimental import pallas as pl
from jax.experimental.pallas import tpu as pltpu
from jax.sharding import PartitionSpec as P

STEPS = 4
ROWS_SENT = 136
MESH = pl.DeviceIdType.MESH
SIDES = ((0, 1), (0, -1), (1, 1), (1, -1), (-1, 1), (-1, -1))
NT = (((1,), (1,)), ((), ()))
BF = jnp.bfloat16
F32 = jnp.float32


def split_two(x):
    hi = x.astype(BF)
    return hi, (x - hi.astype(F32)).astype(BF)


def pack_kernel(tiles, cap, tile_ref, cell_ref, frac_ref, value_ref, prec_ref, out_ref, pay_ref, slot_ref):
    lev, count = value_ref.shape
    tile = tile_ref[...]
    named = (lax.broadcasted_iota(jnp.int32, (tiles, count), 0) == tile).astype(F32)
    width = 256
    upper = (
        lax.broadcasted_iota(jnp.int32, (width, width), 0)
        < lax.broadcasted_iota(jnp.int32, (width, width), 1)
    ).astype(F32).astype(BF)
    carry = jnp.zeros((tiles, 1), F32)
    for first in range(0, count, width):
        part = named[:, first : first + width]
        before = jnp.dot(part.astype(BF), upper, preferred_element_type=F32) + carry
        rank = jnp.sum(before * part, axis=0, keepdims=True)
        slot_ref[:, first : first + width] = (
            tile[:, first : first + width] * cap + rank.astype(jnp.int32)
        )
        carry = carry + jnp.sum(part, axis=1, keepdims=True)
    tail = jnp.concatenate(
        [frac_ref[...], cell_ref[...].astype(F32), jnp.zeros((13, count), F32)], 0
    )
    at = 0
    for piece in (value_ref[...], prec_ref[...], tail):
        hi, lo = split_two(piece)
        n = piece.shape[0]
        pay_ref[at : at + n, :] = hi
        pay_ref[144 + at : 144 + at + n, :] = lo
        at += n
    group = 256 // cap
    slots = slot_ref[...]

    def body(g, _):
        ids = lax.broadcasted_iota(jnp.int32, (256, count), 0) + g * 256
        hot = (ids == slots).astype(F32).astype(BF)
        got = lax.dot_general(pay_ref[...], hot, NT, preferred_element_type=F32)
        both = got[:ROWS_SENT] + got[144 : 144 + ROWS_SENT]
        for j in range(group):
            out_ref[g * group + j] = both[:, j * cap : (j + 1) * cap]
        return 0

    lax.fori_loop(0, tiles // group, body, 0)


def main_kernel(
    n_lat, n_lon, send_ref, control_ref, kappa_ref, vert_ref, vert_t_ref, out_ref,
    recv, ext, side, edges, near, coef, wide, s4, a4, row_out, row_in, col_out, col_in,
    ext2, side2, edges2, near2, hots, w8,
    a_send, a_recv, own_sem, lat_send, lat_recv, lon_send, lon_recv,
    ad_send, ad_recv, lat2_send, lat2_recv, lon2_send, lon2_recv,
):
    devices, _, cap = recv.shape
    lev, rows, cols = control_ref.shape
    sent = 2 * lev + 3
    lat, lon = lax.axis_index("lat"), lax.axis_index("lon")
    me = lat * n_lon + lon
    top = lat == n_lat - 1
    bottom = lat == 0

    def to(dy, dx):
        return (lax.rem(lat + dy + n_lat, n_lat), lax.rem(lon + dx + n_lon, n_lon))

    def at_distance(k):
        d, bit = 0, 1
        while bit < devices:
            d = d + bit * lax.rem(me // bit + k // bit, 2)
            bit *= 2
        return d // n_lon, lax.rem(d, n_lon), d

    barrier = pltpu.get_barrier_semaphore()

    def greet(k, _):
        y, x, _d = at_distance(k)
        pl.semaphore_signal(barrier, inc=1, device_id=(y, x), device_id_type=MESH)
        return 0

    lax.fori_loop(1, devices, greet, 0)
    pl.semaphore_wait(barrier, devices - 1)

    def obs_copy(k):
        y, x, d = at_distance(k)
        return pltpu.make_async_remote_copy(
            src_ref=send_ref.at[d, pl.ds(0, sent)], dst_ref=recv.at[k, pl.ds(0, sent)], send_sem=a_send.at[k],
            recv_sem=a_recv.at[k], device_id=(y, x), device_id_type=MESH,
        )

    lane = lax.broadcasted_iota(jnp.int32, (1, cols), 1)

    def edge_blocks(edges_, ext_):
        east = jnp.zeros(edges_.shape[1:], F32)
        west = jnp.zeros(edges_.shape[1:], F32)
        for r in range(rows):
            x = ext_[r + 4]
            a, b = 4 * r, 5 * r
            east = jnp.where((lane >= a) & (lane < a + 4), pltpu.roll(x, (a + 4) % cols, 1), east)
            west = jnp.where((lane >= b) & (lane < b + 5), pltpu.roll(x, b % cols, 1), west)
        edges_[0] = east
        edges_[1] = west

    def halo_copies(ext_, edges_, near_, sems):
        ls, lr, os, orr = sems
        more = ext_.shape[0] - rows - 4
        copies = [
            pltpu.make_async_remote_copy(
                src_ref=ext_.at[pl.ds(4, more)], dst_ref=ext_.at[pl.ds(rows + 4, more)], send_sem=ls.at[0],
                recv_sem=lr.at[0], device_id=to(-1, 0), device_id_type=MESH),
            pltpu.make_async_remote_copy(
                src_ref=ext_.at[pl.ds(rows, 4)], dst_ref=ext_.at[pl.ds(0, 4)], send_sem=ls.at[1],
                recv_sem=lr.at[1], device_id=to(1, 0), device_id_type=MESH),
        ]
        for j, (dy, dx) in enumerate(SIDES):
            copies.append(pltpu.make_async_remote_copy(
                src_ref=edges_.at[0 if dx < 0 else 1], dst_ref=near_.at[j], send_sem=os.at[j], recv_sem=orr.at[j],
                device_id=to(-dy, -dx), device_id_type=MESH))
        return copies

    def build_side(near_, side_):
        for r in range(side_.shape[0]):
            q = r - 4
            dy = 0 if 0 <= q < rows else (-1 if q < 0 else 1)
            rr = q - dy * rows
            east = near_[SIDES.index((dy, 1))]
            west = near_[SIDES.index((dy, -1))]
            side_[r] = jnp.where(
                lane < 5, pltpu.roll(east, (cols - 5 * rr) % cols, 1),
                jnp.where(lane >= cols - 4, pltpu.roll(west, (cols - 4 - 4 * rr) % cols, 1), 0.0))

    def ring(m, s, step):
        shift = 1 if step < 0 else cols - 1
        edge = lane == (0 if step < 0 else cols - 1)
        rm, rs = pltpu.roll(m, shift, 1), pltpu.roll(s, shift, 1)
        return jnp.where(edge, rs, rm), jnp.where(edge, rm, rs)

    def smooth(main_, side_, put):
        def body(b, _):
            lv = pl.ds(pl.multiple_of(b * 8, 8), 8)
            total = main_.shape[0]
            extra = total - rows - 8
            m = [main_[r, lv, :] for r in range(total)]
            s = [side_[r, lv, :] for r in range(total)]
            for step in range(STEPS):
                nm, ns = list(m), list(s)
                for r in range(step + 1, total - 1 - step):
                    em, es = ring(m[r], s[r], 1)
                    wm, ws = ring(m[r], s[r], -1)
                    nm[r] = (coef[0, r] * m[r] + coef[1, r] * em + coef[2, r] * wm
                             + coef[3, r] * m[r + 1] + coef[3, r - 1] * m[r - 1])
                    if step < STEPS - 1 or extra:
                        ns[r] = (coef[4, r] * s[r] + coef[5, r] * es + coef[6, r] * ws
                                 + coef[7, r] * s[r + 1] + coef[7, r - 1] * s[r - 1])
                m, s = nm, ns
            put(lv, m[4 : 4 + rows + extra], s[4 : 4 + rows + extra])
            return 0

        lax.fori_loop(0, lev // 8, body, 0)

    zero6 = jnp.zeros((6, cols), F32)
    for r in range(rows):
        ext[r + 4, 0:lev, :] = control_ref[:, r, :]
        north = kappa_ref[1, r : r + 1, :]
        if r == rows - 1:
            north = jnp.where(top, 0.0, north)
        ext[r + 4, lev : lev + 8, :] = jnp.concatenate([kappa_ref[0, r : r + 1, :], north, zero6], 0)
    edge_blocks(edges, ext)
    first = halo_copies(ext, edges, near, (lat_send, lat_recv, lon_send, lon_recv))
    for c in first:
        c.start()

    def start_obs(k, _):
        obs_copy(k).start()
        return 0

    lax.fori_loop(1, devices, start_obs, 0)
    own = pltpu.make_async_copy(send_ref.at[me], recv.at[0], own_sem)
    own.start()
    for c in first:
        c.wait()
    build_side(near, side)

    def spread(x):
        return jnp.broadcast_to(x, (8, cols))

    for r in range(rows + 9):
        km, ks = ext[r, lev : lev + 8, :], side[r, lev : lev + 8, :]
        em, es = spread(km[0:1]), spread(ks[0:1])
        wm, ws = ring(em, es, -1)
        nm, ns = spread(km[1:2]), spread(ks[1:2])
        coef[1, r], coef[2, r], coef[3, r] = em, wm, nm
        coef[5, r], coef[6, r], coef[7, r] = es, ws, ns
        if r:
            coef[0, r] = 1.0 - em - wm - nm - coef[3, r - 1]
            coef[4, r] = 1.0 - es - ws - ns - coef[7, r - 1]

    def put_wide(lv, main_rows, side_rows):
        acc = jnp.zeros((8, cols), F32)
        for r in range(rows + 1):
            wide[lv, r * cols : (r + 1) * cols] = main_rows[r]
            acc = jnp.where(lane == r, pltpu.roll(side_rows[r], r, 1), acc)
        wide[lv, (rows + 1) * cols : (rows + 2) * cols] = acc

    smooth(ext, side, put_wide)
    wide[...] = jnp.dot(vert_ref[...], wide[...], precision=lax.Precision.HIGHEST, preferred_element_type=F32)

    def row(r):
        return wide[:, r * cols : (r + 1) * cols]

    def trio(sign, sems, semr):
        return [
            pltpu.make_async_remote_copy(
                src_ref=row_out, dst_ref=row_in, send_sem=sems.at[0], recv_sem=semr.at[0],
                device_id=to(sign, 0), device_id_type=MESH),
            pltpu.make_async_remote_copy(
                src_ref=col_out, dst_ref=col_in.at[0], send_sem=sems.at[1], recv_sem=semr.at[1],
                device_id=to(0, sign), device_id_type=MESH),
            pltpu.make_async_remote_copy(
                src_ref=col_out, dst_ref=col_in.at[1], send_sem=sems.at[2], recv_sem=semr.at[2],
                device_id=to(sign, sign), device_id_type=MESH),
        ]

    last_row = jnp.where(top, 0.0, row(rows))
    east_col = jnp.where(top & (lane == rows), 0.0, row(rows + 1))

    def put_s4(corner, r, x):
        hi, lo = split_two(x)
        s4[corner * lev : (corner + 1) * lev, r * cols : (r + 1) * cols] = hi
        s4[(corner + 4) * lev : (corner + 5) * lev, r * cols : (r + 1) * cols] = lo

    for r in range(rows + 1):
        x = row(r) if r < rows else last_row
        over = pltpu.roll(east_col, cols - 1 - r, 1)
        e = jnp.where(lane == cols - 1, over, pltpu.roll(x, cols - 1, 1))
        if r < rows:
            put_s4(0, r, x)
            put_s4(1, r, e)
        if r:
            put_s4(2, r - 1, x)
            put_s4(3, r - 1, e)

    a4[...] = jnp.zeros_like(a4)
    own.wait()
    group = max(1, 256 // cap)

    width = group * cap
    inner = hots.shape[1] // width

    def work(batch, _):
        lax.fori_loop(0, inner, lambda i, c: one_group(batch * inner + i, i), 0)
        a4[...] += (lax.dot_general(w8[: 4 * lev], hots[...], NT, preferred_element_type=F32)
                    + lax.dot_general(w8[4 * lev :], hots[...], NT, preferred_element_type=F32))
        return 0

    def one_group(g, i):
        for j in range(group):
            k = g * group + j

            @pl.when(k > 0)
            def _():
                obs_copy(k).wait_recv()

        got = jnp.concatenate([recv[g * group + j] for j in range(group)], 1)
        fx, fy = got[2 * lev : 2 * lev + 1], got[2 * lev + 1 : 2 * lev + 2]
        cell = got[2 * lev + 2 : 2 * lev + 3].astype(jnp.int32)
        hot = (lax.broadcasted_iota(jnp.int32, (rows * cols, width), 0) == cell).astype(F32).astype(BF)
        m4 = jnp.dot(s4[...], hot, preferred_element_type=F32)
        shares = ((1.0 - fx) * (1.0 - fy), fx * (1.0 - fy), (1.0 - fx) * fy, fx * fy)
        model = jnp.zeros((lev, width), F32)
        for c, w in enumerate(shares):
            model = model + w * (m4[c * lev : (c + 1) * lev] + m4[(c + 4) * lev : (c + 5) * lev])
        weighted = got[lev : 2 * lev] * (model - got[:lev])
        hi, lo = split_two(jnp.concatenate([w * weighted for w in shares], 0))
        at = pl.ds(pl.multiple_of(i * width, width), width)
        hots[:, at] = hot
        w8[: 4 * lev, at] = hi
        w8[4 * lev :, at] = lo
        return 0

    lax.fori_loop(0, devices // (group * inner), work, 0)

    def part(c, r):
        return a4[c * lev : (c + 1) * lev, r * cols : (r + 1) * cols]

    here, above, packed = [], [], jnp.zeros((lev, cols), F32)
    for r in range(rows):
        e0, e1 = pltpu.roll(part(1, r), 1, 1), pltpu.roll(part(3, r), 1, 1)
        here.append(part(0, r) + jnp.where(lane == 0, 0.0, e0))
        above.append(part(2, r) + jnp.where(lane == 0, 0.0, e1))
        packed = packed + jnp.where(lane == r, pltpu.roll(e0, r, 1), 0.0)
        packed = packed + jnp.where(lane == r + 1, pltpu.roll(e1, r + 1, 1), 0.0)
        wide[:, r * cols : (r + 1) * cols] = here[r] + above[r - 1] if r else here[r]
    row_out[...] = above[rows - 1]
    col_out[...] = packed
    third = trio(1, ad_send, ad_recv)
    for c in third:
        c.start()
    for c in third:
        c.wait()
    wide[:, 0:cols] += (jnp.where(bottom, 0.0, row_in[...])
                        + jnp.where((lane == 0) & jnp.logical_not(bottom), pltpu.roll(col_in[1], cols - rows, 1), 0.0))
    for r in range(rows):
        wide[:, r * cols : (r + 1) * cols] += jnp.where(
            lane == 0, pltpu.roll(col_in[0], (cols - r) % cols, 1), 0.0)
    back = jnp.dot(vert_t_ref[...], wide[:, : rows * cols], precision=lax.Precision.HIGHEST, preferred_element_type=F32)
    for r in range(rows):
        ext2[r + 4] = back[:, r * cols : (r + 1) * cols]
    edge_blocks(edges2, ext2)
    fourth = halo_copies(ext2, edges2, near2, (lat2_send, lat2_recv, lon2_send, lon2_recv))
    for c in fourth:
        c.start()
    for c in fourth:
        c.wait()
    build_side(near2, side2)

    def put_out(lv, main_rows, _side_rows):
        for r in range(rows):
            out_ref[lv, r, :] = main_rows[r]

    smooth(ext2, side2, put_out)

    def end_obs(k, _):
        obs_copy(k).wait_send()
        return 0

    lax.fori_loop(1, devices, end_obs, 0)


def per_device(control, kappa, vert_sqrt, obs_tile, obs_cell, obs_frac, obs_value, obs_precision):
    lev, rows, cols = control.shape
    n_lat, n_lon = lax.axis_size("lat"), lax.axis_size("lon")
    devices = n_lat * n_lon
    count = obs_cell.shape[0]
    cap = 2 * count // devices
    vmem = pl.BlockSpec(memory_space=pltpu.VMEM)
    send = pl.pallas_call(
        functools.partial(pack_kernel, devices, cap),
        out_shape=jax.ShapeDtypeStruct((devices, ROWS_SENT, cap), F32),
        in_specs=[vmem] * 5,
        out_specs=vmem,
        scratch_shapes=[pltpu.VMEM((288, count), BF), pltpu.VMEM((1, count), jnp.int32)],
        compiler_params=pltpu.CompilerParams(vmem_limit_bytes=48 * 2**20),
        name="pack",
    )(obs_tile.reshape(1, count), obs_cell.reshape(1, count), obs_frac, obs_value, obs_precision)
    dma = pltpu.SemaphoreType.DMA
    smoothed = pl.pallas_call(
        functools.partial(main_kernel, n_lat, n_lon),
        out_shape=jax.ShapeDtypeStruct((lev, rows, cols), F32),
        in_specs=[pl.BlockSpec(memory_space=pl.ANY)] + [vmem] * 4,
        out_specs=vmem,
        scratch_shapes=[
            pltpu.VMEM((devices, ROWS_SENT, cap), F32),
            pltpu.VMEM((rows + 9, lev + 8, cols), F32),
            pltpu.VMEM((rows + 9, lev + 8, cols), F32),
            pltpu.VMEM((2, lev + 8, cols), F32),
            pltpu.VMEM((6, lev + 8, cols), F32),
            pltpu.VMEM((8, rows + 9, 8, cols), F32),
            pltpu.VMEM((lev, (rows + 2) * cols), F32),
            pltpu.VMEM((8 * lev, rows * cols), BF),
            pltpu.VMEM((4 * lev, rows * cols), F32),
            pltpu.VMEM((lev, cols), F32),
            pltpu.VMEM((lev, cols), F32),
            pltpu.VMEM((lev, cols), F32),
            pltpu.VMEM((2, lev, cols), F32),
            pltpu.VMEM((rows + 8, lev, cols), F32),
            pltpu.VMEM((rows + 8, lev, cols), F32),
            pltpu.VMEM((2, lev, cols), F32),
            pltpu.VMEM((6, lev, cols), F32),
            pltpu.VMEM((rows * cols, 1024), BF),
            pltpu.VMEM((8 * lev, 1024), BF),
            dma((devices,)), dma((devices,)), dma,
            dma((2,)), dma((2,)), dma((6,)), dma((6,)),
            dma((3,)), dma((3,)),
            dma((2,)), dma((2,)), dma((6,)), dma((6,)),
        ],
        compiler_params=pltpu.CompilerParams(
            collective_id=0, has_side_effects=True, vmem_limit_bytes=48 * 2**20),
        name="main",
    )(send, control, kappa, vert_sqrt, vert_sqrt.T)
    return control + smoothed


def solution(mesh):
    in_specs = (
        P(None, "lat", "lon"), P(None, "lat", "lon"), P(), P(("lat", "lon"), None), P(("lat", "lon")),
        P(None, ("lat", "lon")), P(None, ("lat", "lon")), P(None, ("lat", "lon")),
    )
    return jax.shard_map(
        per_device, mesh=mesh, in_specs=in_specs, out_specs=P(None, "lat", "lon"), check_vma=False
    )
```

```python
import functools

import jax
import jax.numpy as jnp
from jax import lax
from jax.experimental import pallas as pl
from jax.experimental.pallas import tpu as pltpu
from jax.sharding import PartitionSpec as P

STEPS = 4
ROWS_SENT = 136
MESH = pl.DeviceIdType.MESH
SIDES = ((0, 1), (0, -1), (1, 1), (1, -1), (-1, 1), (-1, -1))
NT = (((1,), (1,)), ((), ()))
BF = jnp.bfloat16
F32 = jnp.float32


def split_two(x):
    hi = x.astype(BF)
    return hi, (x - hi.astype(F32)).astype(BF)


def three_products(a, b):
    n = a.shape[0]
    ah, al = split_two(a)
    bh, bl = split_two(b)
    both = jnp.dot(jnp.concatenate([ah, al], 0), bh, preferred_element_type=F32)
    return both[:n] + both[n:] + jnp.dot(ah, bl, preferred_element_type=F32)


def pack_kernel(tiles, cap, tile_ref, cell_ref, frac_ref, value_ref, prec_ref, out_ref, pay_ref, slot_ref):
    lev, count = value_ref.shape
    tile = tile_ref[...]
    named = (lax.broadcasted_iota(jnp.int32, (tiles, count), 0) == tile).astype(F32)
    width = 256
    upper = (
        lax.broadcasted_iota(jnp.int32, (width, width), 0)
        < lax.broadcasted_iota(jnp.int32, (width, width), 1)
    ).astype(F32).astype(BF)
    carry = jnp.zeros((tiles, 1), F32)
    for first in range(0, count, width):
        part = named[:, first : first + width]
        before = jnp.dot(part.astype(BF), upper, preferred_element_type=F32) + carry
        rank = jnp.sum(before * part, axis=0, keepdims=True)
        slot_ref[:, first : first + width] = (
            tile[:, first : first + width] * cap + rank.astype(jnp.int32)
        )
        carry = carry + jnp.sum(part, axis=1, keepdims=True)
    tail = jnp.concatenate(
        [frac_ref[...], cell_ref[...].astype(F32), jnp.zeros((13, count), F32)], 0
    )
    at = 0
    for piece in (value_ref[...], prec_ref[...], tail):
        hi, lo = split_two(piece)
        n = piece.shape[0]
        pay_ref[at : at + n, :] = hi
        pay_ref[144 + at : 144 + at + n, :] = lo
        at += n
    group = 256 // cap
    slots = slot_ref[...]

    def body(g, _):
        ids = lax.broadcasted_iota(jnp.int32, (256, count), 0) + g * 256
        hot = (ids == slots).astype(F32).astype(BF)
        got = lax.dot_general(pay_ref[...], hot, NT, preferred_element_type=F32)
        both = got[:ROWS_SENT] + got[144 : 144 + ROWS_SENT]
        for j in range(group):
            out_ref[g * group + j] = both[:, j * cap : (j + 1) * cap]
        return 0

    lax.fori_loop(0, tiles // group, body, 0)


def main_kernel(
    n_lat, n_lon, send_ref, control_ref, kappa_ref, vert_ref, vert_t_ref, out_ref,
    recv, ext, side, edges, near, coef, wide, s4, a4, row_out, row_in, col_out, col_in,
    ext2, side2, edges2, near2, hots, w8,
    a_send, a_recv, own_sem, lat_send, lat_recv, lon_send, lon_recv,
    ad_send, ad_recv, lat2_send, lat2_recv, lon2_send, lon2_recv,
):
    devices, _, cap = recv.shape
    lev, rows, cols = control_ref.shape
    sent = 2 * lev + 3
    lat, lon = lax.axis_index("lat"), lax.axis_index("lon")
    me = lat * n_lon + lon
    top = lat == n_lat - 1
    bottom = lat == 0

    def to(dy, dx):
        return (lax.rem(lat + dy + n_lat, n_lat), lax.rem(lon + dx + n_lon, n_lon))

    def at_distance(k):
        d, bit = 0, 1
        while bit < devices:
            d = d + bit * lax.rem(me // bit + k // bit, 2)
            bit *= 2
        return d // n_lon, lax.rem(d, n_lon), d

    barrier = pltpu.get_barrier_semaphore()

    def greet(k, _):
        y, x, _d = at_distance(k)
        pl.semaphore_signal(barrier, inc=1, device_id=(y, x), device_id_type=MESH)
        return 0

    lax.fori_loop(1, devices, greet, 0)

    def obs_copy(k):
        y, x, d = at_distance(k)
        return pltpu.make_async_remote_copy(
            src_ref=send_ref.at[d, pl.ds(0, sent)], dst_ref=recv.at[k, pl.ds(0, sent)], send_sem=a_send.at[k],
            recv_sem=a_recv.at[k], device_id=(y, x), device_id_type=MESH,
        )

    lane = lax.broadcasted_iota(jnp.int32, (1, cols), 1)

    def edge_blocks(edges_, ext_):
        east = jnp.zeros(edges_.shape[1:], F32)
        west = jnp.zeros(edges_.shape[1:], F32)
        for r in range(rows):
            x = ext_[r + 4]
            a, b = 4 * r, 5 * r
            east = jnp.where((lane >= a) & (lane < a + 4), pltpu.roll(x, (a + 4) % cols, 1), east)
            west = jnp.where((lane >= b) & (lane < b + 5), pltpu.roll(x, b % cols, 1), west)
        edges_[0] = east
        edges_[1] = west

    def halo_copies(ext_, edges_, near_, sems):
        ls, lr, os, orr = sems
        more = ext_.shape[0] - rows - 4
        copies = [
            pltpu.make_async_remote_copy(
                src_ref=ext_.at[pl.ds(4, more)], dst_ref=ext_.at[pl.ds(rows + 4, more)], send_sem=ls.at[0],
                recv_sem=lr.at[0], device_id=to(-1, 0), device_id_type=MESH),
            pltpu.make_async_remote_copy(
                src_ref=ext_.at[pl.ds(rows, 4)], dst_ref=ext_.at[pl.ds(0, 4)], send_sem=ls.at[1],
                recv_sem=lr.at[1], device_id=to(1, 0), device_id_type=MESH),
        ]
        for j, (dy, dx) in enumerate(SIDES):
            copies.append(pltpu.make_async_remote_copy(
                src_ref=edges_.at[0 if dx < 0 else 1], dst_ref=near_.at[j], send_sem=os.at[j], recv_sem=orr.at[j],
                device_id=to(-dy, -dx), device_id_type=MESH))
        return copies

    def build_side(near_, side_):
        for r in range(side_.shape[0]):
            q = r - 4
            dy = 0 if 0 <= q < rows else (-1 if q < 0 else 1)
            rr = q - dy * rows
            east = near_[SIDES.index((dy, 1))]
            west = near_[SIDES.index((dy, -1))]
            side_[r] = jnp.where(
                lane < 5, pltpu.roll(east, (cols - 5 * rr) % cols, 1),
                jnp.where(lane >= cols - 4, pltpu.roll(west, (cols - 4 - 4 * rr) % cols, 1), 0.0))

    def ring(m, s, step):
        shift = 1 if step < 0 else cols - 1
        edge = lane == (0 if step < 0 else cols - 1)
        rm, rs = pltpu.roll(m, shift, 1), pltpu.roll(s, shift, 1)
        return jnp.where(edge, rs, rm), jnp.where(edge, rm, rs)

    def smooth(main_, side_, put):
        def body(b, _):
            lv = pl.ds(pl.multiple_of(b * 8, 8), 8)
            total = main_.shape[0]
            extra = total - rows - 8
            m = [main_[r, lv, :] for r in range(total)]
            s = [side_[r, lv, :] for r in range(total)]
            for step in range(STEPS):
                nm, ns = list(m), list(s)
                for r in range(step + 1, total - 1 - step):
                    em, es = ring(m[r], s[r], 1)
                    wm, ws = ring(m[r], s[r], -1)
                    nm[r] = (coef[0, r] * m[r] + coef[1, r] * em + coef[2, r] * wm
                             + coef[3, r] * m[r + 1] + coef[3, r - 1] * m[r - 1])
                    if step < STEPS - 1 or extra:
                        ns[r] = (coef[4, r] * s[r] + coef[5, r] * es + coef[6, r] * ws
                                 + coef[7, r] * s[r + 1] + coef[7, r - 1] * s[r - 1])
                m, s = nm, ns
            put(lv, m[4 : 4 + rows + extra], s[4 : 4 + rows + extra])
            return 0

        lax.fori_loop(0, lev // 8, body, 0)

    zero6 = jnp.zeros((6, cols), F32)
    for r in range(rows):
        ext[r + 4, 0:lev, :] = control_ref[:, r, :]
        north = kappa_ref[1, r : r + 1, :]
        if r == rows - 1:
            north = jnp.where(top, 0.0, north)
        ext[r + 4, lev : lev + 8, :] = jnp.concatenate([kappa_ref[0, r : r + 1, :], north, zero6], 0)
    edge_blocks(edges, ext)
    pl.semaphore_wait(barrier, devices - 1)
    first = halo_copies(ext, edges, near, (lat_send, lat_recv, lon_send, lon_recv))
    for c in first:
        c.start()

    def start_obs(k, _):
        obs_copy(k).start()
        return 0

    lax.fori_loop(1, devices, start_obs, 0)
    own = pltpu.make_async_copy(send_ref.at[me], recv.at[0], own_sem)
    own.start()
    for c in first:
        c.wait()
    build_side(near, side)

    def spread(x):
        return jnp.broadcast_to(x, (8, cols))

    for r in range(rows + 9):
        km, ks = ext[r, lev : lev + 8, :], side[r, lev : lev + 8, :]
        em, es = spread(km[0:1]), spread(ks[0:1])
        wm, ws = ring(em, es, -1)
        nm, ns = spread(km[1:2]), spread(ks[1:2])
        coef[1, r], coef[2, r], coef[3, r] = em, wm, nm
        coef[5, r], coef[6, r], coef[7, r] = es, ws, ns
        if r:
            coef[0, r] = 1.0 - em - wm - nm - coef[3, r - 1]
            coef[4, r] = 1.0 - es - ws - ns - coef[7, r - 1]

    def put_wide(lv, main_rows, side_rows):
        acc = jnp.zeros((8, cols), F32)
        for r in range(rows + 1):
            wide[lv, r * cols : (r + 1) * cols] = main_rows[r]
            acc = jnp.where(lane == r, pltpu.roll(side_rows[r], r, 1), acc)
        wide[lv, (rows + 1) * cols : (rows + 2) * cols] = acc

    smooth(ext, side, put_wide)
    wide[...] = three_products(vert_ref[...], wide[...])

    def row(r):
        return wide[:, r * cols : (r + 1) * cols]

    def trio(sign, sems, semr):
        return [
            pltpu.make_async_remote_copy(
                src_ref=row_out, dst_ref=row_in, send_sem=sems.at[0], recv_sem=semr.at[0],
                device_id=to(sign, 0), device_id_type=MESH),
            pltpu.make_async_remote_copy(
                src_ref=col_out, dst_ref=col_in.at[0], send_sem=sems.at[1], recv_sem=semr.at[1],
                device_id=to(0, sign), device_id_type=MESH),
            pltpu.make_async_remote_copy(
                src_ref=col_out, dst_ref=col_in.at[1], send_sem=sems.at[2], recv_sem=semr.at[2],
                device_id=to(sign, sign), device_id_type=MESH),
        ]

    last_row = jnp.where(top, 0.0, row(rows))
    east_col = jnp.where(top & (lane == rows), 0.0, row(rows + 1))

    def put_s4(corner, r, x):
        hi, lo = split_two(x)
        s4[corner * lev : (corner + 1) * lev, r * cols : (r + 1) * cols] = hi
        s4[(corner + 4) * lev : (corner + 5) * lev, r * cols : (r + 1) * cols] = lo

    for r in range(rows + 1):
        x = row(r) if r < rows else last_row
        over = pltpu.roll(east_col, cols - 1 - r, 1)
        e = jnp.where(lane == cols - 1, over, pltpu.roll(x, cols - 1, 1))
        if r < rows:
            put_s4(0, r, x)
            put_s4(1, r, e)
        if r:
            put_s4(2, r - 1, x)
            put_s4(3, r - 1, e)

    a4[...] = jnp.zeros_like(a4)
    own.wait()
    group = max(1, 256 // cap)

    width = group * cap
    inner = hots.shape[1] // width

    def work(batch, _):
        lax.fori_loop(0, inner, lambda i, c: one_group(batch * inner + i, i), 0)
        a4[...] += (lax.dot_general(w8[: 4 * lev], hots[...], NT, preferred_element_type=F32)
                    + lax.dot_general(w8[4 * lev :], hots[...], NT, preferred_element_type=F32))
        return 0

    def one_group(g, i):
        for j in range(group):
            k = g * group + j

            @pl.when(k > 0)
            def _():
                obs_copy(k).wait_recv()

        got = jnp.concatenate([recv[g * group + j] for j in range(group)], 1)
        fx, fy = got[2 * lev : 2 * lev + 1], got[2 * lev + 1 : 2 * lev + 2]
        cell = got[2 * lev + 2 : 2 * lev + 3].astype(jnp.int32)
        hot = (lax.broadcasted_iota(jnp.int32, (rows * cols, width), 0) == cell).astype(F32).astype(BF)
        m4 = jnp.dot(s4[...], hot, preferred_element_type=F32)
        shares = ((1.0 - fx) * (1.0 - fy), fx * (1.0 - fy), (1.0 - fx) * fy, fx * fy)
        model = jnp.zeros((lev, width), F32)
        for c, w in enumerate(shares):
            model = model + w * (m4[c * lev : (c + 1) * lev] + m4[(c + 4) * lev : (c + 5) * lev])
        weighted = got[lev : 2 * lev] * (model - got[:lev])
        hi, lo = split_two(jnp.concatenate([w * weighted for w in shares], 0))
        at = pl.ds(pl.multiple_of(i * width, width), width)
        hots[:, at] = hot
        w8[: 4 * lev, at] = hi
        w8[4 * lev :, at] = lo
        return 0

    lax.fori_loop(0, devices // (group * inner), work, 0)

    def part(c, r):
        return a4[c * lev : (c + 1) * lev, r * cols : (r + 1) * cols]

    here, above, packed = [], [], jnp.zeros((lev, cols), F32)
    for r in range(rows):
        e0, e1 = pltpu.roll(part(1, r), 1, 1), pltpu.roll(part(3, r), 1, 1)
        here.append(part(0, r) + jnp.where(lane == 0, 0.0, e0))
        above.append(part(2, r) + jnp.where(lane == 0, 0.0, e1))
        packed = packed + jnp.where(lane == r, pltpu.roll(e0, r, 1), 0.0)
        packed = packed + jnp.where(lane == r + 1, pltpu.roll(e1, r + 1, 1), 0.0)
        wide[:, r * cols : (r + 1) * cols] = here[r] + above[r - 1] if r else here[r]
    row_out[...] = above[rows - 1]
    col_out[...] = packed
    third = trio(1, ad_send, ad_recv)
    for c in third:
        c.start()
    for c in third:
        c.wait()
    wide[:, 0:cols] += (jnp.where(bottom, 0.0, row_in[...])
                        + jnp.where((lane == 0) & jnp.logical_not(bottom), pltpu.roll(col_in[1], cols - rows, 1), 0.0))
    for r in range(rows):
        wide[:, r * cols : (r + 1) * cols] += jnp.where(
            lane == 0, pltpu.roll(col_in[0], (cols - r) % cols, 1), 0.0)
    back = three_products(vert_t_ref[...], wide[:, : rows * cols])
    for r in range(rows):
        ext2[r + 4] = back[:, r * cols : (r + 1) * cols]
    edge_blocks(edges2, ext2)
    fourth = halo_copies(ext2, edges2, near2, (lat2_send, lat2_recv, lon2_send, lon2_recv))
    for c in fourth:
        c.start()
    for c in fourth:
        c.wait()
    build_side(near2, side2)

    def put_out(lv, main_rows, _side_rows):
        for r in range(rows):
            out_ref[lv, r, :] = main_rows[r]

    smooth(ext2, side2, put_out)

    def end_obs(k, _):
        obs_copy(k).wait_send()
        return 0

    lax.fori_loop(1, devices, end_obs, 0)


def per_device(control, kappa, vert_sqrt, obs_tile, obs_cell, obs_frac, obs_value, obs_precision):
    lev, rows, cols = control.shape
    n_lat, n_lon = lax.axis_size("lat"), lax.axis_size("lon")
    devices = n_lat * n_lon
    count = obs_cell.shape[0]
    cap = 2 * count // devices
    vmem = pl.BlockSpec(memory_space=pltpu.VMEM)
    send = pl.pallas_call(
        functools.partial(pack_kernel, devices, cap),
        out_shape=jax.ShapeDtypeStruct((devices, ROWS_SENT, cap), F32),
        in_specs=[vmem] * 5,
        out_specs=vmem,
        scratch_shapes=[pltpu.VMEM((288, count), BF), pltpu.VMEM((1, count), jnp.int32)],
        compiler_params=pltpu.CompilerParams(vmem_limit_bytes=48 * 2**20),
        name="pack",
    )(obs_tile.reshape(1, count), obs_cell.reshape(1, count), obs_frac, obs_value, obs_precision)
    dma = pltpu.SemaphoreType.DMA
    smoothed = pl.pallas_call(
        functools.partial(main_kernel, n_lat, n_lon),
        out_shape=jax.ShapeDtypeStruct((lev, rows, cols), F32),
        in_specs=[pl.BlockSpec(memory_space=pl.ANY)] + [vmem] * 4,
        out_specs=vmem,
        scratch_shapes=[
            pltpu.VMEM((devices, ROWS_SENT, cap), F32),
            pltpu.VMEM((rows + 9, lev + 8, cols), F32),
            pltpu.VMEM((rows + 9, lev + 8, cols), F32),
            pltpu.VMEM((2, lev + 8, cols), F32),
            pltpu.VMEM((6, lev + 8, cols), F32),
            pltpu.VMEM((8, rows + 9, 8, cols), F32),
            pltpu.VMEM((lev, (rows + 2) * cols), F32),
            pltpu.VMEM((8 * lev, rows * cols), BF),
            pltpu.VMEM((4 * lev, rows * cols), F32),
            pltpu.VMEM((lev, cols), F32),
            pltpu.VMEM((lev, cols), F32),
            pltpu.VMEM((lev, cols), F32),
            pltpu.VMEM((2, lev, cols), F32),
            pltpu.VMEM((rows + 8, lev, cols), F32),
            pltpu.VMEM((rows + 8, lev, cols), F32),
            pltpu.VMEM((2, lev, cols), F32),
            pltpu.VMEM((6, lev, cols), F32),
            pltpu.VMEM((rows * cols, 512), BF),
            pltpu.VMEM((8 * lev, 512), BF),
            dma((devices,)), dma((devices,)), dma,
            dma((2,)), dma((2,)), dma((6,)), dma((6,)),
            dma((3,)), dma((3,)),
            dma((2,)), dma((2,)), dma((6,)), dma((6,)),
        ],
        compiler_params=pltpu.CompilerParams(
            collective_id=0, has_side_effects=True, vmem_limit_bytes=48 * 2**20),
        name="main",
    )(send, control, kappa, vert_sqrt, vert_sqrt.T)
    return control + smoothed


def solution(mesh):
    in_specs = (
        P(None, "lat", "lon"), P(None, "lat", "lon"), P(), P(("lat", "lon"), None), P(("lat", "lon")),
        P(None, ("lat", "lon")), P(None, ("lat", "lon")), P(None, ("lat", "lon")),
    )
    return jax.shard_map(
        per_device, mesh=mesh, in_specs=in_specs, out_specs=P(None, "lat", "lon"), check_vma=False
    )
```
